32 devices in a mesh: atom: 2 (over x), slab: 16 (over z, y, core).
Axes of the slice: x: 2, y: 2, z: 4, core: 2. Of those that a mesh axis runs over, the one named last changes fastest.
Arguments:
- atom_log_density: float32 [2, 256, 64, 512], P('atom', 'slab'), may hold values from -123 to 121
- prior_log_scaling: float32 [2, 256, 64, 512], P('atom', 'slab'), may hold values from -5 to 115
- atom_cotangent_rows: float32 [2, 256, 64, 512], P('atom', 'slab'), may hold values from -6 to 6
- barycenter_cotangent: float32 [256, 64, 512], P('slab'), may hold values from -6 to 6
- weights: float32 [2], replicated, may hold values from 0.2 to 1
- band: int32 [3], replicated, may hold values from 1 to 8, as said below
- slot_atom_index: int32 [2], replicated, may hold values from 0 to 1, each once
Outputs:
- log_atom_gradient: float32 [2, 256, 64, 512], P('atom', 'slab')
- weight_grad: float32 [2], replicated
The draws below stay inside these ranges and needn't reach their ends.
Inputs may be any that keep to these rules, and one draw needn't show every extreme that they name: `band`: at least one entry equals 8. `slot_atom_index`: each atom is held in exactly one slot.
All inputs are finite; a program needn't handle non-finite values.
Results may differ from the reference program's by a relative error of at most 0.0003.
Values sent between devices are 32-bit elements; how exact they have to be, the bound alone decides.
A program may use at most 64 MiB of HBM per device.

```python
import jax
import jax.numpy as jnp
from jax import lax

NX = 512
NY = 64
PLANES = 16
BAND_MAX = 8
ATOMS = 2
NZ = 256


def draw_atom_log_density(key, part):
    first_key, second_key, third_key = jax.random.split(jax.random.fold_in(key, 23), 3)
    rough = jax.random.uniform(first_key, (ATOMS, NZ, NY, NX), jnp.float32, -3.0, 1.0)
    ranks = jax.random.permutation(second_key, ATOMS).astype(jnp.float32)
    levels = -115.0 + 230.0 * ranks / max(ATOMS - 1, 1)
    slab_offset = jax.random.uniform(third_key, (ATOMS, NZ // PLANES, 1, 1), jnp.float32, -5.0, 5.0)
    slab_offset = jnp.repeat(slab_offset, PLANES, axis=1)
    return (rough + slab_offset + levels[:, None, None, None]).astype(jnp.float32)


def draw_prior_log_scaling(key, part):
    first_key, second_key, third_key = jax.random.split(jax.random.fold_in(key, 11), 3)
    rough = jax.random.uniform(first_key, (ATOMS, NZ, NY, NX), jnp.float32, -3.0, 3.0)
    slab_level = jax.random.uniform(third_key, (ATOMS, NZ // PLANES, 1, 1), jnp.float32, 0.0, 8.0)
    slab_level = jnp.repeat(slab_level, PLANES, axis=1)
    offset = jax.random.uniform(second_key, (ATOMS, 1, 1, 1), jnp.float32, -2.0, 2.0)
    return (rough + slab_level + offset).astype(jnp.float32)


def draw_band(key, part):
    raw_bits = jax.random.bits(key, (4,), jnp.uint32)
    widths = (raw_bits[:3] % BAND_MAX).astype(jnp.int32) + 1
    chosen = (raw_bits[3] % 3).astype(jnp.int32)
    return jnp.where(jnp.arange(3, dtype=jnp.int32) == chosen, jnp.int32(BAND_MAX), widths).astype(jnp.int32)


def shard_levels(own_key, dims, cuts, least, largest):
    def one(axis_at, parts):
        steps = jax.random.uniform(jax.random.fold_in(jax.random.fold_in(own_key, 6), axis_at), (parts,), jnp.float32, least / len(cuts), largest / len(cuts))
        return jnp.repeat(jnp.exp(steps), dims[axis_at] // parts).reshape((-1,) + (1,) * (len(dims) - axis_at - 1))

    factor_of = one(*cuts[0])
    for cut in cuts[1:]:
        factor_of = factor_of * one(*cut)
    return factor_of


def centred(key, extent, scale, most, cuts=(), held_as=jnp.bfloat16):
    result = scale * jax.random.normal(key, extent, jnp.float32)
    if cuts:
        result = result * shard_levels(key, extent, cuts, -0.22, 0.18)
    return jnp.clip(result, -most, most).astype(held_as)


def setup_inputs(seed: int = 0) -> dict:
    arg_keys = jax.random.split(jax.random.key(seed), 8)
    atom_log_density = draw_atom_log_density(jax.random.fold_in(arg_keys[7], 71), 0)
    prior_log_scaling = draw_prior_log_scaling(jax.random.fold_in(arg_keys[7], 71), 0)
    atom_cotangent_rows = centred(arg_keys[2], (ATOMS, NZ, NY, NX), 1.0, 6.0, ((0, 2), (1, 16)), jnp.float32)
    barycenter_cotangent = centred(arg_keys[3], (NZ, NY, NX), 1.0, 6.0, ((0, 16),), jnp.float32)
    weights = jnp.clip(jax.random.uniform(arg_keys[4], (ATOMS,), jnp.float32, 0.2, 1.0), 0.2, 1.0)
    band = draw_band(jax.random.fold_in(arg_keys[7], 71), 0)
    slot_atom_index = jax.random.permutation(arg_keys[6], ATOMS).astype(jnp.int32)
    return {"atom_log_density": atom_log_density, "prior_log_scaling": prior_log_scaling, "atom_cotangent_rows": atom_cotangent_rows, "barycenter_cotangent": barycenter_cotangent, "weights": weights, "band": band, "slot_atom_index": slot_atom_index}


def kernel_table(count, half):
    positions = jnp.arange(count, dtype=jnp.int32)
    offsets = positions[:, None] - positions[None, :]
    spread = offsets.astype(jnp.float32)
    values = jnp.exp(-2.0 * spread * spread / (BAND_MAX * BAND_MAX))
    return jnp.where(jnp.abs(offsets) <= half, values, jnp.float32(0.0))


def blur_three(field, kernel_columns, kernel_rows, kern_z):
    high = lax.Precision.HIGHEST
    section = jnp.einsum('zyx,xv->zyv', field, kernel_columns, precision=high)
    section = jnp.einsum('zyx,yv->zvx', section, kernel_rows, precision=high)
    return jnp.einsum('zyx,zw->wyx', section, kern_z, precision=high)


def reference(atom_log_density, prior_log_scaling, atom_cotangent_rows, barycenter_cotangent, weights, band, slot_atom_index):
    kernel_columns = kernel_table(NX, band[0])
    kernel_rows = kernel_table(NY, band[1])
    kern_z = kernel_table(NZ, band[2])
    summed = barycenter_cotangent + jnp.sum(atom_cotangent_rows, axis=0)
    slot_mixing_weight = weights[slot_atom_index]

    def single_entry(items):
        log_atom, log_scal, cot_atom, weight_one = items
        peak_gradient = jnp.max(log_scal)
        first_entry = blur_three(jnp.exp(log_scal - peak_gradient), kernel_columns, kernel_rows, kern_z)
        potential = log_atom - (jnp.log(first_entry) + peak_gradient)
        peak_f = jnp.max(potential)
        shifted = jnp.exp(potential - peak_f)
        second = blur_three(shifted, kernel_columns, kernel_rows, kern_z)
        mixed = jnp.log(second) + peak_f
        adjoint = weight_one * summed - cot_atom
        gradient = shifted * blur_three(adjoint / second, kernel_columns, kernel_rows, kern_z)
        total_one = jnp.sum(summed * mixed) / (NX * NY * NZ)
        return gradient, total_one

    log_atom_gradient, slot_sum_totals = lax.map(single_entry, (atom_log_density, prior_log_scaling, atom_cotangent_rows, slot_mixing_weight))
    weight_grad = jnp.zeros((ATOMS,), jnp.float32).at[slot_atom_index].set(slot_sum_totals)
    return log_atom_gradient, weight_grad
```

```python
import functools

import jax
import jax.numpy as jnp
from jax import lax
from jax.experimental import pallas as pl
from jax.experimental.pallas import tpu as pltpu
from jax.sharding import PartitionSpec as P

BAND_MAX = 8
ROWS = 16
MESH = pl.DeviceIdType.MESH
F32 = jnp.float32
BF16 = jnp.bfloat16


def tap(offset):
    spread = offset.astype(F32)
    return jnp.exp(-2.0 * spread * spread / (BAND_MAX * BAND_MAX))


def split(value):
    high = value.astype(BF16)
    return high, (value - high.astype(F32)).astype(BF16)


def dot3(a_high, a_low, b_high, b_low):
    dot = functools.partial(jnp.dot, preferred_element_type=F32)
    return dot(a_high, b_high) + (dot(a_high, b_low) + dot(a_low, b_high))


def kernel(
    swap, slabs, planes, rows, cols,
    dens_hbm, prior_hbm, cot_hbm, bary_hbm, weights_ref, band_ref, slot_ref,
    out_hbm, part_ref,
    own, halo, cot, bary, other, xbuf, zbuf, ybuf, obuf, mine, msg, kx, ky, zmax,
    load_sem, out_sem, hsend, hrecv, msend, mrecv, csend, crecv,
):
    chunks = rows // ROWS
    me = lax.axis_index("slab")
    atom = lax.axis_index("atom")
    right = lax.rem(me + 1, slabs)
    left = lax.rem(me + slabs - 1, slabs)
    has_left = me > 0
    has_right = me < slabs - 1

    loads = [
        pltpu.make_async_copy(src, dst, load_sem.at[i])
        for i, (src, dst) in enumerate(
            [
                (prior_hbm.at[0], own.at[0]),
                (dens_hbm.at[0], own.at[1]),
                (cot_hbm.at[0], cot),
                (bary_hbm, bary),
            ]
        )
    ]
    for load in loads:
        load.start()

    barrier = pltpu.get_barrier_semaphore()

    @pl.when(has_left)
    def _():
        pl.semaphore_signal(barrier, inc=1, device_id=(atom, left), device_id_type=MESH)

    @pl.when(has_right)
    def _():
        pl.semaphore_signal(barrier, inc=1, device_id=(atom, right), device_id_type=MESH)

    if swap:
        pl.semaphore_signal(barrier, inc=1, device_id=(1 - atom, me), device_id_type=MESH)

    def rows_of(c):
        return pl.ds(pl.multiple_of(c * ROWS, ROWS), ROWS)

    def halo_copy(stage, way, c):
        first = planes - BAND_MAX if way == 0 else 0
        return pltpu.make_async_remote_copy(
            src_ref=own.at[stage, pl.ds(first, BAND_MAX), rows_of(c), :],
            dst_ref=halo.at[stage, way, :, rows_of(c), :],
            send_sem=hsend.at[stage, way, c],
            recv_sem=hrecv.at[stage, way, c],
            device_id=(atom, right if way == 0 else left),
            device_id_type=MESH,
        )

    def msg_copy(stage, way):
        return pltpu.make_async_remote_copy(
            src_ref=mine.at[stage],
            dst_ref=msg.at[stage, way],
            send_sem=msend.at[stage, way],
            recv_sem=mrecv.at[stage, way],
            device_id=(atom, right if way == 0 else left),
            device_id_type=MESH,
        )

    def cot_copy(c):
        return pltpu.make_async_remote_copy(
            src_ref=cot_hbm.at[0, :, rows_of(c), :],
            dst_ref=other.at[:, rows_of(c), :],
            send_sem=csend.at[c],
            recv_sem=crecv.at[c],
            device_id=(1 - atom, me),
            device_id_type=MESH,
        )

    there = (has_right, has_left)
    comes = (has_left, has_right)

    def send(stage, c):
        for way in range(2):
            @pl.when(there[way])
            def _():
                halo_copy(stage, way, c).start()

    def send_msg(stage, value):
        mine[stage] = jnp.full((8, 128), value, F32)
        for way in range(2):
            @pl.when(there[way])
            def _():
                msg_copy(stage, way).start()

    def take_msg(stage):
        for way in range(2):
            @pl.when(comes[way])
            def _():
                msg_copy(stage, way).wait_recv()

            @pl.when(jnp.logical_not(comes[way]))
            def _():
                msg[stage, way] = mine[stage]
        return jnp.max(msg[stage, 0]), jnp.max(msg[stage, 1])

    d = lax.broadcasted_iota(jnp.int32, (cols, cols), 0) - lax.broadcasted_iota(jnp.int32, (cols, cols), 1)
    kx[0], kx[1] = split(jnp.where(jnp.abs(d) <= band_ref[0], tap(d), 0.0))
    i = lax.broadcasted_iota(jnp.int32, (8 * ROWS, 16 * ROWS), 0)
    j = lax.broadcasted_iota(jnp.int32, (8 * ROWS, 16 * ROWS), 1)
    d = (j & (2 * ROWS - 1)) - ROWS // 2 - (i & (ROWS - 1))
    same = (i // ROWS) == (j // (2 * ROWS))
    ky[0], ky[1] = split(jnp.where(same & (jnp.abs(d) <= band_ref[1]), tap(d), 0.0))
    xbuf[:, 0:8, :] = jnp.zeros((planes, 8, cols), F32)
    xbuf[:, rows + 8 : rows + 16, :] = jnp.zeros((planes, 8, cols), F32)
    part_ref[...] = jnp.zeros(part_ref.shape, F32)
    for way in range(2):
        @pl.when(jnp.logical_not(comes[way]))
        def _():
            @pl.loop(0, 3)
            def _(stage):
                @pl.loop(0, BAND_MAX)
                def _(p):
                    halo[stage, way, p] = jnp.zeros((rows, cols), F32)

    half = band_ref[2]
    wz = [
        jnp.where(half >= k, tap(jnp.full((8, 128), k, jnp.int32)), 0.0)
        for k in range(BAND_MAX + 1)
    ]

    def zx(stage, c, factors):
        for way in range(2):
            @pl.when(comes[way])
            def _():
                halo_copy(stage, way, c).wait_recv()

        tiles = cols // 128

        @pl.loop(0, tiles * (ROWS // 8))
        def _(t):
            r = pl.multiple_of((t // tiles) * 8, 8)
            at = pl.ds(pl.multiple_of(c * ROWS + r, 8), 8)
            lanes = pl.ds(pl.multiple_of((t % tiles) * 128, 128), 128)
            e = [halo[stage, 0, p, at, lanes] * factors[0] for p in range(BAND_MAX)]
            e += [own[stage, p, at, lanes] * factors[1] for p in range(planes)]
            e += [halo[stage, 1, p, at, lanes] * factors[2] for p in range(BAND_MAX)]
            for p in range(planes):
                total = e[p + 8] * wz[0]
                for k in range(1, BAND_MAX + 1):
                    total = total + (e[p + 8 - k] + e[p + 8 + k]) * wz[k]
                zbuf[p, pl.ds(r, 8), lanes] = total

        high, low = split(zbuf[...].reshape(planes * ROWS, cols))
        res = dot3(high, low, kx[0], kx[1]).reshape(planes, ROWS, cols)
        xbuf[:, pl.ds(pl.multiple_of(c * ROWS + 8, 8), ROWS), :] = res

    def yy(c):
        around = pl.ds(pl.multiple_of(c * ROWS, ROWS), 2 * ROWS)
        for part in range(planes // 8):
            high, low = split(xbuf[part * 8 : part * 8 + 8, around, :].reshape(16 * ROWS, cols))
            ybuf[part * 8 : part * 8 + 8] = dot3(ky[0], ky[1], high, low).reshape(8, ROWS, cols)

    def run(stage, factors, post):
        @pl.loop(0, chunks + 1)
        def _(c):
            @pl.when(c < chunks)
            def _():
                zx(stage, c, factors)

            @pl.when(c > 0)
            def _():
                yy(c - 1)
                post(c - 1)

    def factor(a, b):
        return jnp.exp(jnp.full((8, 128), a - b, F32))

    loads[0].wait()
    zmax[...] = jnp.full((8, cols), -jnp.inf, F32)

    @pl.loop(0, planes)
    def _(p):
        zmax[...] = jnp.maximum(zmax[...], jnp.max(own[0, p].reshape(rows // 8, 8, cols), axis=0))

    m1 = jnp.max(zmax[...])
    count = has_left.astype(jnp.int32) + has_right.astype(jnp.int32) + (1 if swap else 0)
    pl.semaphore_wait(barrier, count)
    send_msg(0, m1)

    @pl.loop(0, chunks)
    def _(c):
        @pl.loop(0, planes)
        def _(p):
            own[0, p, rows_of(c), :] = jnp.exp(own[0, p, rows_of(c), :] - m1)

        send(0, c)

    if swap:
        @pl.loop(0, chunks)
        def _(c):
            cot_copy(c).start()

    m1_left, m1_right = take_msg(0)
    c1 = jnp.maximum(m1, jnp.maximum(m1_left, m1_right))
    loads[1].wait()
    zmax[...] = jnp.full((8, cols), -jnp.inf, F32)

    def post1(c):
        @pl.loop(0, planes)
        def _(p):
            potential = own[1, p, rows_of(c), :] - (jnp.log(ybuf[p]) + c1)
            own[1, p, rows_of(c), :] = potential
            zmax[...] = jnp.maximum(zmax[...], jnp.max(potential.reshape(ROWS // 8, 8, cols), axis=0))

    run(0, [factor(m1_left, c1), factor(m1, c1), factor(m1_right, c1)], post1)

    m2 = jnp.max(zmax[...])
    send_msg(1, m2)

    @pl.loop(0, chunks)
    def _(c):
        @pl.loop(0, planes)
        def _(p):
            own[1, p, rows_of(c), :] = jnp.exp(own[1, p, rows_of(c), :] - m2)

        send(1, c)

    m2_left, m2_right = take_msg(1)
    c2 = jnp.maximum(m2, jnp.maximum(m2_left, m2_right))
    send_msg(2, c2)
    weight = weights_ref[slot_ref[atom]]
    loads[2].wait()
    loads[3].wait()

    def post2(c):
        if swap:
            cot_copy(c).wait_recv()

        @pl.loop(0, planes)
        def _(p):
            cot_here = cot[p, rows_of(c), :]
            summed = bary[p, rows_of(c), :]
            if swap:
                summed = summed + (cot_here + other[p, rows_of(c), :])
            second = ybuf[p]
            product = summed * (jnp.log(second) + c2)
            part_ref[...] += jnp.sum(product.reshape(ROWS // 8, 8, cols), axis=0)
            own[2, p, rows_of(c), :] = (weight * summed - cot_here) / second

        send(2, c)

    run(1, [factor(m2_left, c2), factor(m2, c2), factor(m2_right, c2)], post2)

    c2_left, c2_right = take_msg(2)

    def out_copy(c):
        return pltpu.make_async_copy(
            obuf.at[:, rows_of(c), :], out_hbm.at[0, :, rows_of(c), :], out_sem.at[c]
        )

    def post3(c):
        @pl.loop(0, planes)
        def _(p):
            obuf[p, rows_of(c), :] = own[1, p, rows_of(c), :] * ybuf[p]

        out_copy(c).start()

    run(2, [factor(m2, c2_left), factor(m2, c2), factor(m2, c2_right)], post3)

    @pl.loop(0, chunks)
    def _(c):
        out_copy(c).wait()
        if swap:
            cot_copy(c).wait_send()
        for stage in range(3):
            for way in range(2):
                @pl.when(there[way])
                def _():
                    halo_copy(stage, way, c).wait_send()

    for stage in range(3):
        for way in range(2):
            @pl.when(there[way])
            def _():
                msg_copy(stage, way).wait_send()


def body(dens, prior, cot, bary, weights, band, slot_atom_index):
    held = dens.shape[0]
    assert held == 1
    planes, rows, cols = bary.shape
    slabs = lax.axis_size("slab")
    swap = lax.axis_size("atom") == 2
    chunks = rows // ROWS
    if not swap:
        bary = bary + lax.psum(cot[0], "atom")
    dma = pltpu.SemaphoreType.DMA
    full = pltpu.VMEM((planes, rows, cols), F32)
    grad, part = pl.pallas_call(
        functools.partial(kernel, swap, slabs, planes, rows, cols),
        out_shape=(
            jax.ShapeDtypeStruct(dens.shape, F32),
            jax.ShapeDtypeStruct((8, cols), F32),
        ),
        in_specs=[pl.BlockSpec(memory_space=pl.ANY)] * 4 + [pl.BlockSpec(memory_space=pltpu.SMEM)] * 3,
        out_specs=(pl.BlockSpec(memory_space=pl.ANY), pl.BlockSpec(memory_space=pltpu.VMEM)),
        scratch_shapes=[
            pltpu.VMEM((3, planes, rows, cols), F32),
            pltpu.VMEM((3, 2, BAND_MAX, rows, cols), F32),
            full,
            full,
            full,
            pltpu.VMEM((planes, rows + 16, cols), F32),
            pltpu.VMEM((planes, ROWS, cols), F32),
            pltpu.VMEM((planes, ROWS, cols), F32),
            full,
            pltpu.VMEM((3, 8, 128), F32),
            pltpu.VMEM((3, 2, 8, 128), F32),
            pltpu.VMEM((2, cols, cols), BF16),
            pltpu.VMEM((2, 8 * ROWS, 16 * ROWS), BF16),
            pltpu.VMEM((8, cols), F32),
            dma((4,)),
            dma((chunks,)),
            dma((3, 2, chunks)),
            dma((3, 2, chunks)),
            dma((3, 2)),
            dma((3, 2)),
            dma((chunks,)),
            dma((chunks,)),
        ],
        compiler_params=pltpu.CompilerParams(
            collective_id=0, has_side_effects=True, vmem_limit_bytes=52 * 1024 * 1024
        ),
        name="sinkhorn_reverse",
    )(dens, prior, cot, bary, weights, band, slot_atom_index)
    atom = lax.axis_index("atom")
    slot = lax.dynamic_slice_in_dim(slot_atom_index, atom, 1)
    onehot = (slot == jnp.arange(weights.shape[0], dtype=jnp.int32)).astype(F32)
    weight_grad = lax.psum(onehot * jnp.sum(part), ("atom", "slab")) / (slabs * planes * rows * cols)
    return grad, weight_grad


def solution(mesh):
    return jax.shard_map(
        body,
        mesh=mesh,
        in_specs=(
            P("atom", "slab", None, None),
            P("atom", "slab", None, None),
            P("atom", "slab", None, None),
            P("slab", None, None),
            P(),
            P(),
            P(),
        ),
        out_specs=(P("atom", "slab", None, None), P()),
        check_vma=False,
    )
```

```python
import functools

import jax
import jax.numpy as jnp
from jax import lax
from jax.experimental import pallas as pl
from jax.experimental.pallas import tpu as pltpu
from jax.sharding import PartitionSpec as P

BAND_MAX = 8
ROWS = 16
MESH = pl.DeviceIdType.MESH
F32 = jnp.float32
BF16 = jnp.bfloat16


def tap(offset):
    spread = offset.astype(F32)
    return jnp.exp(-2.0 * spread * spread / (BAND_MAX * BAND_MAX))


def split(value):
    high = value.astype(BF16)
    return high, (value - high.astype(F32)).astype(BF16)


def dot3(a_high, a_low, b_high, b_low):
    dot = functools.partial(jnp.dot, preferred_element_type=F32)
    return dot(a_high, b_high) + (dot(a_high, b_low) + dot(a_low, b_high))


def kernel(
    swap, atoms, slabs, planes, rows, cols,
    dens_hbm, prior_hbm, cot_hbm, bary_hbm, weights_ref, band_ref, slot_ref,
    out_hbm, wgrad_ref,
    own, halo, cot, bary, other, xbuf, zbuf, ybuf, obuf, mine, msg, kx, ky, zmax, part_ref, slab_parts, atom_parts,
    load_sem, out_sem, hsend, hrecv, msend, mrecv, csend, crecv, psend, precv, asend, arecv,
):
    chunks = rows // ROWS
    me = lax.axis_index("slab")
    atom = lax.axis_index("atom")
    right = lax.rem(me + 1, slabs)
    left = lax.rem(me + slabs - 1, slabs)
    has_left = me > 0
    has_right = me < slabs - 1

    loads = [
        pltpu.make_async_copy(src, dst, load_sem.at[i])
        for i, (src, dst) in enumerate(
            [
                (prior_hbm.at[0], own.at[0]),
                (dens_hbm.at[0], own.at[1]),
                (cot_hbm.at[0], cot),
                (bary_hbm, bary),
            ]
        )
    ]
    for load in loads:
        load.start()

    barrier = pltpu.get_barrier_semaphore()

    @pl.loop(1, slabs)
    def _(k):
        pl.semaphore_signal(
            barrier, inc=1, device_id=(atom, lax.rem(me + k, slabs)), device_id_type=MESH
        )

    @pl.loop(1, atoms)
    def _(k):
        pl.semaphore_signal(
            barrier, inc=1, device_id=(lax.rem(atom + k, atoms), me), device_id_type=MESH
        )

    def rows_of(c):
        return pl.ds(pl.multiple_of(c * ROWS, ROWS), ROWS)

    def halo_copy(stage, way, c):
        first = planes - BAND_MAX if way == 0 else 0
        return pltpu.make_async_remote_copy(
            src_ref=own.at[stage, pl.ds(first, BAND_MAX), rows_of(c), :],
            dst_ref=halo.at[stage, way, :, rows_of(c), :],
            send_sem=hsend.at[stage, way, c],
            recv_sem=hrecv.at[stage, way, c],
            device_id=(atom, right if way == 0 else left),
            device_id_type=MESH,
        )

    def msg_copy(stage, way):
        return pltpu.make_async_remote_copy(
            src_ref=mine.at[stage],
            dst_ref=msg.at[stage, way],
            send_sem=msend.at[stage, way],
            recv_sem=mrecv.at[stage, way],
            device_id=(atom, right if way == 0 else left),
            device_id_type=MESH,
        )

    def cot_copy(c):
        return pltpu.make_async_remote_copy(
            src_ref=cot_hbm.at[0, :, rows_of(c), :],
            dst_ref=other.at[:, rows_of(c), :],
            send_sem=csend.at[c],
            recv_sem=crecv.at[c],
            device_id=(1 - atom, me),
            device_id_type=MESH,
        )

    def part_copy(source, target):
        return pltpu.make_async_remote_copy(
            src_ref=slab_parts.at[me],
            dst_ref=slab_parts.at[source],
            send_sem=psend.at[target],
            recv_sem=precv.at[source],
            device_id=(atom, target),
            device_id_type=MESH,
        )

    def atom_copy(source, target):
        return pltpu.make_async_remote_copy(
            src_ref=atom_parts.at[atom],
            dst_ref=atom_parts.at[source],
            send_sem=asend.at[target],
            recv_sem=arecv.at[source],
            device_id=(target, me),
            device_id_type=MESH,
        )

    there = (has_right, has_left)
    comes = (has_left, has_right)

    def send(stage, c):
        for way in range(2):
            @pl.when(there[way])
            def _():
                halo_copy(stage, way, c).start()

    def send_msg(stage, value):
        mine[stage] = jnp.full((8, 128), value, F32)
        for way in range(2):
            @pl.when(there[way])
            def _():
                msg_copy(stage, way).start()

    def take_msg(stage):
        for way in range(2):
            @pl.when(comes[way])
            def _():
                msg_copy(stage, way).wait_recv()

            @pl.when(jnp.logical_not(comes[way]))
            def _():
                msg[stage, way] = mine[stage]
        return jnp.max(msg[stage, 0]), jnp.max(msg[stage, 1])

    d = lax.broadcasted_iota(jnp.int32, (cols, cols), 0) - lax.broadcasted_iota(jnp.int32, (cols, cols), 1)
    kx[0], kx[1] = split(jnp.where(jnp.abs(d) <= band_ref[0], tap(d), 0.0))
    i = lax.broadcasted_iota(jnp.int32, (8 * ROWS, 16 * ROWS), 0)
    j = lax.broadcasted_iota(jnp.int32, (8 * ROWS, 16 * ROWS), 1)
    d = (j & (2 * ROWS - 1)) - ROWS // 2 - (i & (ROWS - 1))
    same = (i // ROWS) == (j // (2 * ROWS))
    ky[0], ky[1] = split(jnp.where(same & (jnp.abs(d) <= band_ref[1]), tap(d), 0.0))
    xbuf[:, 0:8, :] = jnp.zeros((planes, 8, cols), F32)
    xbuf[:, rows + 8 : rows + 16, :] = jnp.zeros((planes, 8, cols), F32)
    part_ref[...] = jnp.zeros(part_ref.shape, F32)
    for way in range(2):
        @pl.when(jnp.logical_not(comes[way]))
        def _():
            @pl.loop(0, 3)
            def _(stage):
                @pl.loop(0, BAND_MAX)
                def _(p):
                    halo[stage, way, p] = jnp.zeros((rows, cols), F32)

    half = band_ref[2]
    wz = [
        jnp.where(half >= k, tap(jnp.full((8, 128), k, jnp.int32)), 0.0)
        for k in range(BAND_MAX + 1)
    ]

    def zx(stage, c, factors):
        for way in range(2):
            @pl.when(comes[way])
            def _():
                halo_copy(stage, way, c).wait_recv()

        tiles = cols // 128

        @pl.loop(0, tiles * (ROWS // 8))
        def _(t):
            r = pl.multiple_of((t // tiles) * 8, 8)
            at = pl.ds(pl.multiple_of(c * ROWS + r, 8), 8)
            lanes = pl.ds(pl.multiple_of((t % tiles) * 128, 128), 128)
            e = [halo[stage, 0, p, at, lanes] * factors[0] for p in range(BAND_MAX)]
            e += [own[stage, p, at, lanes] * factors[1] for p in range(planes)]
            e += [halo[stage, 1, p, at, lanes] * factors[2] for p in range(BAND_MAX)]
            for p in range(planes):
                total = e[p + 8] * wz[0]
                for k in range(1, BAND_MAX + 1):
                    total = total + (e[p + 8 - k] + e[p + 8 + k]) * wz[k]
                zbuf[p, pl.ds(r, 8), lanes] = total

        high, low = split(zbuf[...].reshape(planes * ROWS, cols))
        res = dot3(high, low, kx[0], kx[1]).reshape(planes, ROWS, cols)
        xbuf[:, pl.ds(pl.multiple_of(c * ROWS + 8, 8), ROWS), :] = res

    def yy(c):
        around = pl.ds(pl.multiple_of(c * ROWS, ROWS), 2 * ROWS)
        for part in range(planes // 8):
            high, low = split(xbuf[part * 8 : part * 8 + 8, around, :].reshape(16 * ROWS, cols))
            ybuf[part * 8 : part * 8 + 8] = dot3(ky[0], ky[1], high, low).reshape(8, ROWS, cols)

    def run(stage, factors, post):
        @pl.loop(0, chunks + 1)
        def _(c):
            @pl.when(c < chunks)
            def _():
                zx(stage, c, factors)

            @pl.when(c > 0)
            def _():
                yy(c - 1)
                post(c - 1)

    def factor(a, b):
        return jnp.exp(jnp.full((8, 128), a - b, F32))

    loads[0].wait()
    zmax[...] = jnp.full((8, cols), -jnp.inf, F32)

    @pl.loop(0, planes)
    def _(p):
        zmax[...] = jnp.maximum(zmax[...], jnp.max(own[0, p].reshape(rows // 8, 8, cols), axis=0))

    m1 = jnp.max(zmax[...])
    pl.semaphore_wait(barrier, slabs - 1 + atoms - 1)
    send_msg(0, m1)

    @pl.loop(0, chunks)
    def _(c):
        @pl.loop(0, planes)
        def _(p):
            own[0, p, rows_of(c), :] = jnp.exp(own[0, p, rows_of(c), :] - m1)

        send(0, c)

    if swap:
        @pl.loop(0, chunks)
        def _(c):
            cot_copy(c).start()

    m1_left, m1_right = take_msg(0)
    c1 = jnp.maximum(m1, jnp.maximum(m1_left, m1_right))
    loads[1].wait()
    zmax[...] = jnp.full((8, cols), -jnp.inf, F32)

    def post1(c):
        @pl.loop(0, planes)
        def _(p):
            potential = own[1, p, rows_of(c), :] - (jnp.log(ybuf[p]) + c1)
            own[1, p, rows_of(c), :] = potential
            zmax[...] = jnp.maximum(zmax[...], jnp.max(potential.reshape(ROWS // 8, 8, cols), axis=0))

    run(0, [factor(m1_left, c1), factor(m1, c1), factor(m1_right, c1)], post1)

    m2 = jnp.max(zmax[...])
    send_msg(1, m2)

    @pl.loop(0, chunks)
    def _(c):
        @pl.loop(0, planes)
        def _(p):
            own[1, p, rows_of(c), :] = jnp.exp(own[1, p, rows_of(c), :] - m2)

        send(1, c)

    m2_left, m2_right = take_msg(1)
    c2 = jnp.maximum(m2, jnp.maximum(m2_left, m2_right))
    send_msg(2, c2)
    weight = weights_ref[slot_ref[atom]]
    loads[2].wait()
    loads[3].wait()

    def post2(c):
        if swap:
            cot_copy(c).wait_recv()

        @pl.loop(0, planes)
        def _(p):
            cot_here = cot[p, rows_of(c), :]
            summed = bary[p, rows_of(c), :]
            if swap:
                summed = summed + (cot_here + other[p, rows_of(c), :])
            second = ybuf[p]
            product = summed * (jnp.log(second) + c2)
            part_ref[...] += jnp.sum(product.reshape(ROWS // 8, 8, cols), axis=0)
            own[2, p, rows_of(c), :] = (weight * summed - cot_here) / second

        send(2, c)

    run(1, [factor(m2_left, c2), factor(m2, c2), factor(m2_right, c2)], post2)

    slab_parts[me] = sum(part_ref[:, k * 128 : (k + 1) * 128] for k in range(cols // 128))

    @pl.loop(1, slabs)
    def _(k):
        part_copy(me, lax.rem(me + k, slabs)).start()

    def share():
        @pl.loop(1, slabs)
        def _(k):
            other_slab = lax.rem(me + k, slabs)
            part_copy(other_slab, other_slab).wait_recv()

        atom_parts[atom] = jnp.sum(slab_parts[...], axis=0) / (slabs * planes * rows * cols)

        @pl.loop(1, atoms)
        def _(k):
            atom_copy(atom, lax.rem(atom + k, atoms)).start()

    c2_left, c2_right = take_msg(2)

    def out_copy(c):
        return pltpu.make_async_copy(
            obuf.at[:, rows_of(c), :], out_hbm.at[0, :, rows_of(c), :], out_sem.at[c]
        )

    def post3(c):
        @pl.loop(0, planes)
        def _(p):
            obuf[p, rows_of(c), :] = own[1, p, rows_of(c), :] * ybuf[p]

        out_copy(c).start()

        @pl.when(c == chunks - 2)
        def _():
            share()

    run(2, [factor(m2, c2_left), factor(m2, c2), factor(m2, c2_right)], post3)

    @pl.loop(0, chunks)
    def _(c):
        out_copy(c).wait()
        if swap:
            cot_copy(c).wait_send()
        for stage in range(3):
            for way in range(2):
                @pl.when(there[way])
                def _():
                    halo_copy(stage, way, c).wait_send()

    for stage in range(3):
        for way in range(2):
            @pl.when(there[way])
            def _():
                msg_copy(stage, way).wait_send()

    @pl.loop(1, slabs)
    def _(k):
        target = lax.rem(me + k, slabs)
        part_copy(me, target).wait_send()

    @pl.loop(1, atoms)
    def _(k):
        other_atom = lax.rem(atom + k, atoms)
        atom_copy(atom, other_atom).wait_send()
        atom_copy(other_atom, other_atom).wait_recv()

    totals = [jnp.sum(atom_parts[k]) for k in range(atoms)]
    for j in range(atoms):
        wgrad_ref[j] = sum(jnp.where(slot_ref[k] == j, totals[k], 0.0) for k in range(atoms))


def body(dens, prior, cot, bary, weights, band, slot_atom_index):
    held = dens.shape[0]
    assert held == 1
    planes, rows, cols = bary.shape
    slabs = lax.axis_size("slab")
    atoms = lax.axis_size("atom")
    swap = atoms == 2
    chunks = rows // ROWS
    if not swap:
        bary = bary + lax.psum(cot[0], "atom")
    dma = pltpu.SemaphoreType.DMA
    full = pltpu.VMEM((planes, rows, cols), F32)
    return pl.pallas_call(
        functools.partial(kernel, swap, atoms, slabs, planes, rows, cols),
        out_shape=(
            jax.ShapeDtypeStruct(dens.shape, F32),
            jax.ShapeDtypeStruct((atoms,), F32),
        ),
        in_specs=[pl.BlockSpec(memory_space=pl.ANY)] * 4 + [pl.BlockSpec(memory_space=pltpu.SMEM)] * 3,
        out_specs=(pl.BlockSpec(memory_space=pl.ANY), pl.BlockSpec(memory_space=pltpu.SMEM)),
        scratch_shapes=[
            pltpu.VMEM((3, planes, rows, cols), F32),
            pltpu.VMEM((3, 2, BAND_MAX, rows, cols), F32),
            full,
            full,
            full,
            pltpu.VMEM((planes, rows + 16, cols), F32),
            pltpu.VMEM((planes, ROWS, cols), F32),
            pltpu.VMEM((planes, ROWS, cols), F32),
            full,
            pltpu.VMEM((3, 8, 128), F32),
            pltpu.VMEM((3, 2, 8, 128), F32),
            pltpu.VMEM((2, cols, cols), BF16),
            pltpu.VMEM((2, 8 * ROWS, 16 * ROWS), BF16),
            pltpu.VMEM((8, cols), F32),
            pltpu.VMEM((8, cols), F32),
            pltpu.VMEM((slabs, 8, 128), F32),
            pltpu.VMEM((atoms, 8, 128), F32),
            dma((4,)),
            dma((chunks,)),
            dma((3, 2, chunks)),
            dma((3, 2, chunks)),
            dma((3, 2)),
            dma((3, 2)),
            dma((chunks,)),
            dma((chunks,)),
            dma((slabs,)),
            dma((slabs,)),
            dma((atoms,)),
            dma((atoms,)),
        ],
        compiler_params=pltpu.CompilerParams(
            collective_id=0, has_side_effects=True, vmem_limit_bytes=52 * 1024 * 1024
        ),
        name="sinkhorn_reverse",
    )(dens, prior, cot, bary, weights, band, slot_atom_index)


def solution(mesh):
    return jax.shard_map(
        body,
        mesh=mesh,
        in_specs=(
            P("atom", "slab", None, None),
            P("atom", "slab", None, None),
            P("atom", "slab", None, None),
            P("slab", None, None),
            P(),
            P(),
            P(),
        ),
        out_specs=(P("atom", "slab", None, None), P()),
        check_vma=False,
    )
```

```python
import functools

import jax
import jax.numpy as jnp
from jax import lax
from jax.experimental import pallas as pl
from jax.experimental.pallas import tpu as pltpu
from jax.sharding import PartitionSpec as P

BAND_MAX = 8
ROWS = 16
STEP = 2
MESH = pl.DeviceIdType.MESH
F32 = jnp.float32
BF16 = jnp.bfloat16


def tap(offset):
    spread = offset.astype(F32)
    return jnp.exp(-2.0 * spread * spread / (BAND_MAX * BAND_MAX))


def split(value):
    high = value.astype(BF16)
    return high, (value - high.astype(F32)).astype(BF16)


def dot3(a_high, a_low, b_high, b_low):
    dot = functools.partial(jnp.dot, preferred_element_type=F32)
    return dot(a_high, b_high) + (dot(a_high, b_low) + dot(a_low, b_high))


def kernel(
    reach, swap, atoms, slabs, planes, rows, cols,
    dens_hbm, prior_hbm, cot_hbm, bary_hbm, weights_hbm, band_hbm, slot_hbm,
    out_hbm, wgrad_ref,
    own, halo, cot, bary, other, xbuf, zbuf, ybuf, obuf, mine, msg, kx, ky, zmax, part_ref, slab_parts, atom_parts,
    weights_ref, band_ref, slot_ref,
    load_sem, out_sem, hsend, hrecv, msend, mrecv, csend, crecv, psend, precv, asend, arecv,
):
    chunks = rows // ROWS
    me = lax.axis_index("slab")
    atom = lax.axis_index("atom")
    right = lax.rem(me + 1, slabs)
    left = lax.rem(me + slabs - 1, slabs)
    has_left = me > 0
    has_right = me < slabs - 1

    loads = [
        pltpu.make_async_copy(src, dst, load_sem.at[i])
        for i, (src, dst) in enumerate(
            [
                (band_hbm, band_ref),
                (weights_hbm, weights_ref),
                (slot_hbm, slot_ref),
                (prior_hbm.at[0], own.at[0]),
                (dens_hbm.at[0], own.at[1]),
                (cot_hbm.at[0], cot),
                (bary_hbm, bary),
            ]
        )
    ]
    for load in loads:
        load.start()

    barrier = pltpu.get_barrier_semaphore()

    @pl.loop(1, slabs)
    def _(k):
        pl.semaphore_signal(
            barrier, inc=1, device_id=(atom, lax.rem(me + k, slabs)), device_id_type=MESH
        )

    @pl.loop(1, atoms)
    def _(k):
        pl.semaphore_signal(
            barrier, inc=1, device_id=(lax.rem(atom + k, atoms), me), device_id_type=MESH
        )

    def rows_of(c):
        return pl.ds(pl.multiple_of(c * ROWS, ROWS), ROWS)

    def halo_copy(stage, way, c):
        first = planes - reach if way == 0 else 0
        return pltpu.make_async_remote_copy(
            src_ref=own.at[stage, pl.ds(first, reach), rows_of(c), :],
            dst_ref=halo.at[stage, way, :, rows_of(c), :],
            send_sem=hsend.at[stage, way, c],
            recv_sem=hrecv.at[stage, way, c],
            device_id=(atom, right if way == 0 else left),
            device_id_type=MESH,
        )

    def msg_copy(stage, way):
        return pltpu.make_async_remote_copy(
            src_ref=mine.at[stage],
            dst_ref=msg.at[stage, way],
            send_sem=msend.at[stage, way],
            recv_sem=mrecv.at[stage, way],
            device_id=(atom, right if way == 0 else left),
            device_id_type=MESH,
        )

    def cot_copy(c):
        return pltpu.make_async_remote_copy(
            src_ref=cot_hbm.at[0, :, rows_of(c), :],
            dst_ref=other.at[:, rows_of(c), :],
            send_sem=csend.at[c],
            recv_sem=crecv.at[c],
            device_id=(1 - atom, me),
            device_id_type=MESH,
        )

    def part_copy(source, target):
        return pltpu.make_async_remote_copy(
            src_ref=slab_parts.at[me],
            dst_ref=slab_parts.at[source],
            send_sem=psend.at[target],
            recv_sem=precv.at[source],
            device_id=(atom, target),
            device_id_type=MESH,
        )

    def atom_copy(source, target):
        return pltpu.make_async_remote_copy(
            src_ref=atom_parts.at[atom],
            dst_ref=atom_parts.at[source],
            send_sem=asend.at[target],
            recv_sem=arecv.at[source],
            device_id=(target, me),
            device_id_type=MESH,
        )

    there = (has_right, has_left)
    comes = (has_left, has_right)

    def send(stage, c):
        for way in range(2):
            @pl.when(there[way])
            def _():
                halo_copy(stage, way, c).start()

    def send_msg(stage, value):
        mine[stage] = jnp.full((8, 128), value, F32)
        for way in range(2):
            @pl.when(there[way])
            def _():
                msg_copy(stage, way).start()

    def take_msg(stage):
        for way in range(2):
            @pl.when(comes[way])
            def _():
                msg_copy(stage, way).wait_recv()

            @pl.when(jnp.logical_not(comes[way]))
            def _():
                msg[stage, way] = mine[stage]
        return jnp.max(msg[stage, 0]), jnp.max(msg[stage, 1])

    for load in loads[:3]:
        load.wait()

    d = lax.broadcasted_iota(jnp.int32, (cols, cols), 0) - lax.broadcasted_iota(jnp.int32, (cols, cols), 1)
    kx[0], kx[1] = split(jnp.where(jnp.abs(d) <= band_ref[0], tap(d), 0.0))
    i = lax.broadcasted_iota(jnp.int32, (8 * ROWS, 16 * ROWS), 0)
    j = lax.broadcasted_iota(jnp.int32, (8 * ROWS, 16 * ROWS), 1)
    d = (j & (2 * ROWS - 1)) - ROWS // 2 - (i & (ROWS - 1))
    same = (i // ROWS) == (j // (2 * ROWS))
    ky[0], ky[1] = split(jnp.where(same & (jnp.abs(d) <= band_ref[1]), tap(d), 0.0))
    xbuf[:, 0:8, :] = jnp.zeros((planes, 8, cols), F32)
    xbuf[:, rows + 8 : rows + 16, :] = jnp.zeros((planes, 8, cols), F32)
    part_ref[...] = jnp.zeros(part_ref.shape, F32)
    for way in range(2):
        @pl.when(jnp.logical_not(comes[way]))
        def _():
            @pl.loop(0, 3)
            def _(stage):
                @pl.loop(0, reach)
                def _(p):
                    halo[stage, way, p] = jnp.zeros((rows, cols), F32)

    half = band_ref[2]
    wz = [
        jnp.where(half >= k, tap(jnp.full((8, 128), k, jnp.int32)), 0.0)
        for k in range(reach + 1)
    ]

    def zx(stage, c, factors):
        for way in range(2):
            @pl.when(comes[way])
            def _():
                halo_copy(stage, way, c).wait_recv()

        tiles = cols // 128

        @pl.loop(0, tiles * (ROWS // 8))
        def _(t):
            r = pl.multiple_of((t // tiles) * 8, 8)
            at = pl.ds(pl.multiple_of(c * ROWS + r, 8), 8)
            lanes = pl.ds(pl.multiple_of((t % tiles) * 128, 128), 128)
            e = [halo[stage, 0, p, at, lanes] * factors[0] for p in range(reach)]
            e += [own[stage, p, at, lanes] * factors[1] for p in range(planes)]
            e += [halo[stage, 1, p, at, lanes] * factors[2] for p in range(reach)]
            for p in range(planes):
                total = e[p + reach] * wz[0]
                for k in range(1, reach + 1):
                    total = total + (e[p + reach - k] + e[p + reach + k]) * wz[k]
                zbuf[p, pl.ds(r, 8), lanes] = total

        high, low = split(zbuf[...].reshape(planes * ROWS, cols))
        res = dot3(high, low, kx[0], kx[1]).reshape(planes, ROWS, cols)
        xbuf[:, pl.ds(pl.multiple_of(c * ROWS + 8, 8), ROWS), :] = res

    def yy(c):
        around = pl.ds(pl.multiple_of(c * ROWS, ROWS), 2 * ROWS)
        for part in range(planes // 8):
            high, low = split(xbuf[part * 8 : part * 8 + 8, around, :].reshape(16 * ROWS, cols))
            ybuf[part * 8 : part * 8 + 8] = dot3(ky[0], ky[1], high, low).reshape(8, ROWS, cols)

    def run(stage, factors, post):
        @pl.loop(0, chunks + 1)
        def _(c):
            @pl.when(c < chunks)
            def _():
                zx(stage, c, factors)

            @pl.when(c > 0)
            def _():
                yy(c - 1)
                post(c - 1)

    def factor(a, b):
        return jnp.exp(jnp.full((8, 128), a - b, F32))

    loads[3].wait()
    zmax[...] = jnp.full((8, cols), -jnp.inf, F32)

    @pl.loop(0, planes)
    def _(p):
        zmax[...] = jnp.maximum(zmax[...], jnp.max(own[0, p].reshape(rows // 8, 8, cols), axis=0))

    m1 = jnp.max(zmax[...])
    pl.semaphore_wait(barrier, slabs - 1 + atoms - 1)
    send_msg(0, m1)

    @pl.loop(0, chunks)
    def _(c):
        @pl.loop(0, planes)
        def _(p):
            own[0, p, rows_of(c), :] = jnp.exp(own[0, p, rows_of(c), :] - m1)

        send(0, c)

    if swap:
        @pl.loop(0, chunks)
        def _(c):
            cot_copy(c).start()

    m1_left, m1_right = take_msg(0)
    c1 = jnp.maximum(m1, jnp.maximum(m1_left, m1_right))
    loads[4].wait()
    zmax[...] = jnp.full((8, cols), -jnp.inf, F32)

    def post1(c):
        @pl.loop(0, planes)
        def _(p):
            potential = own[1, p, rows_of(c), :] - (jnp.log(ybuf[p]) + c1)
            own[1, p, rows_of(c), :] = potential
            zmax[...] = jnp.maximum(zmax[...], jnp.max(potential.reshape(ROWS // 8, 8, cols), axis=0))

    run(0, [factor(m1_left, c1), factor(m1, c1), factor(m1_right, c1)], post1)

    m2 = jnp.max(zmax[...])
    send_msg(1, m2)

    @pl.loop(0, chunks)
    def _(c):
        @pl.loop(0, planes)
        def _(p):
            own[1, p, rows_of(c), :] = jnp.exp(own[1, p, rows_of(c), :] - m2)

        send(1, c)

    m2_left, m2_right = take_msg(1)
    c2 = jnp.maximum(m2, jnp.maximum(m2_left, m2_right))
    send_msg(2, c2)
    weight = weights_ref[slot_ref[atom]]
    loads[5].wait()
    loads[6].wait()

    def post2(c):
        if swap:
            cot_copy(c).wait_recv()

        @pl.loop(0, planes)
        def _(p):
            cot_here = cot[p, rows_of(c), :]
            summed = bary[p, rows_of(c), :]
            if swap:
                summed = summed + (cot_here + other[p, rows_of(c), :])
            second = ybuf[p]
            product = summed * (jnp.log(second) + c2)
            part_ref[...] += jnp.sum(product.reshape(ROWS // 8, 8, cols), axis=0)
            own[2, p, rows_of(c), :] = (weight * summed - cot_here) / second

        send(2, c)

    run(1, [factor(m2_left, c2), factor(m2, c2), factor(m2_right, c2)], post2)

    slab_parts[me] = sum(part_ref[:, k * 128 : (k + 1) * 128] for k in range(cols // 128))

    @pl.loop(1, slabs)
    def _(k):
        part_copy(me, lax.rem(me + k, slabs)).start()

    def share():
        @pl.loop(1, slabs)
        def _(k):
            other_slab = lax.rem(me + k, slabs)
            part_copy(other_slab, other_slab).wait_recv()

        atom_parts[atom] = jnp.sum(slab_parts[...], axis=0) / (slabs * planes * rows * cols)

        @pl.loop(1, atoms)
        def _(k):
            atom_copy(atom, lax.rem(atom + k, atoms)).start()

    c2_left, c2_right = take_msg(2)

    def out_copy(c):
        return pltpu.make_async_copy(
            obuf.at[:, rows_of(c), :], out_hbm.at[0, :, rows_of(c), :], out_sem.at[c]
        )

    def post3(c):
        @pl.loop(0, planes)
        def _(p):
            obuf[p, rows_of(c), :] = own[1, p, rows_of(c), :] * ybuf[p]

        out_copy(c).start()

        @pl.when(c == chunks - 2)
        def _():
            share()

    run(2, [factor(m2, c2_left), factor(m2, c2), factor(m2, c2_right)], post3)

    @pl.loop(0, chunks)
    def _(c):
        out_copy(c).wait()
        if swap:
            cot_copy(c).wait_send()
        for stage in range(3):
            for way in range(2):
                @pl.when(there[way])
                def _():
                    halo_copy(stage, way, c).wait_send()

    for stage in range(3):
        for way in range(2):
            @pl.when(there[way])
            def _():
                msg_copy(stage, way).wait_send()

    @pl.loop(1, slabs)
    def _(k):
        target = lax.rem(me + k, slabs)
        part_copy(me, target).wait_send()

    @pl.loop(1, atoms)
    def _(k):
        other_atom = lax.rem(atom + k, atoms)
        atom_copy(atom, other_atom).wait_send()
        atom_copy(other_atom, other_atom).wait_recv()

    totals = [jnp.sum(atom_parts[k]) for k in range(atoms)]
    for j in range(atoms):
        wgrad_ref[j] = sum(jnp.where(slot_ref[k] == j, totals[k], 0.0) for k in range(atoms))


def body(dens, prior, cot, bary, weights, band, slot_atom_index):
    swap = lax.axis_size("atom") == 2
    if not swap:
        bary = bary + lax.psum(cot[0], "atom")
    steps = BAND_MAX // STEP
    which = sum((band[2] > STEP * k).astype(jnp.int32) for k in range(1, steps))
    return lax.switch(
        which,
        [functools.partial(reverse, STEP * (k + 1)) for k in range(steps)],
        dens, prior, cot, bary, weights, band, slot_atom_index,
    )


def reverse(reach, dens, prior, cot, bary, weights, band, slot_atom_index):
    held = dens.shape[0]
    assert held == 1
    planes, rows, cols = bary.shape
    slabs = lax.axis_size("slab")
    atoms = lax.axis_size("atom")
    swap = atoms == 2
    chunks = rows // ROWS
    dma = pltpu.SemaphoreType.DMA
    full = pltpu.VMEM((planes, rows, cols), F32)
    return pl.pallas_call(
        functools.partial(kernel, reach, swap, atoms, slabs, planes, rows, cols),
        out_shape=(
            jax.ShapeDtypeStruct(dens.shape, F32),
            jax.ShapeDtypeStruct((atoms,), F32),
        ),
        in_specs=[pl.BlockSpec(memory_space=pl.ANY)] * 7,
        out_specs=(pl.BlockSpec(memory_space=pl.ANY), pl.BlockSpec(memory_space=pltpu.SMEM)),
        scratch_shapes=[
            pltpu.VMEM((3, planes, rows, cols), F32),
            pltpu.VMEM((3, 2, reach, rows, cols), F32),
            full,
            full,
            full,
            pltpu.VMEM((planes, rows + 16, cols), F32),
            pltpu.VMEM((planes, ROWS, cols), F32),
            pltpu.VMEM((planes, ROWS, cols), F32),
            full,
            pltpu.VMEM((3, 8, 128), F32),
            pltpu.VMEM((3, 2, 8, 128), F32),
            pltpu.VMEM((2, cols, cols), BF16),
            pltpu.VMEM((2, 8 * ROWS, 16 * ROWS), BF16),
            pltpu.VMEM((8, cols), F32),
            pltpu.VMEM((8, cols), F32),
            pltpu.VMEM((slabs, 8, 128), F32),
            pltpu.VMEM((atoms, 8, 128), F32),
            pltpu.SMEM((atoms,), F32),
            pltpu.SMEM((3,), jnp.int32),
            pltpu.SMEM((atoms,), jnp.int32),
            dma((7,)),
            dma((chunks,)),
            dma((3, 2, chunks)),
            dma((3, 2, chunks)),
            dma((3, 2)),
            dma((3, 2)),
            dma((chunks,)),
            dma((chunks,)),
            dma((slabs,)),
            dma((slabs,)),
            dma((atoms,)),
            dma((atoms,)),
        ],
        compiler_params=pltpu.CompilerParams(
            collective_id=reach, has_side_effects=True, vmem_limit_bytes=52 * 1024 * 1024
        ),
        name=f"sinkhorn_reach_{reach}",
    )(dens, prior, cot, bary, weights, band, slot_atom_index)


def solution(mesh):
    return jax.shard_map(
        body,
        mesh=mesh,
        in_specs=(
            P("atom", "slab", None, None),
            P("atom", "slab", None, None),
            P("atom", "slab", None, None),
            P("slab", None, None),
            P(),
            P(),
            P(),
        ),
        out_specs=(P("atom", "slab", None, None), P()),
        check_vma=False,
    )
```

```python
import functools

import jax
import jax.numpy as jnp
from jax import lax
from jax.experimental import pallas as pl
from jax.experimental.pallas import tpu as pltpu
from jax.sharding import PartitionSpec as P

BAND_MAX = 8
ROWS = 16
STEP = 2
MESH = pl.DeviceIdType.MESH
F32 = jnp.float32
BF16 = jnp.bfloat16


def tap(offset):
    spread = offset.astype(F32)
    return jnp.exp(-2.0 * spread * spread / (BAND_MAX * BAND_MAX))


def split(value):
    high = value.astype(BF16)
    return high, (value - high.astype(F32)).astype(BF16)


def dot(a, b):
    return jnp.dot(a, b, preferred_element_type=F32)


def kernel(
    reach, swap, atoms, slabs, planes, rows, cols,
    dens_hbm, prior_hbm, cot_hbm, bary_hbm, weights_hbm, band_hbm, slot_hbm,
    out_hbm, wgrad_ref,
    own, halo, cot, bary, other, xbuf, zbuf, ybuf, obuf, mine, msg, kx, ky, zmax, part_ref, slab_parts, atom_parts,
    weights_ref, band_ref, slot_ref, fac, fin,
    load_sem, out_sem, hsend, hrecv, msend, mrecv, csend, crecv, psend, precv, asend, arecv,
):
    chunks = rows // ROWS
    me = lax.axis_index("slab")
    atom = lax.axis_index("atom")
    right = lax.rem(me + 1, slabs)
    left = lax.rem(me + slabs - 1, slabs)
    has_left = me > 0
    has_right = me < slabs - 1

    loads = [
        pltpu.make_async_copy(src, dst, load_sem.at[i])
        for i, (src, dst) in enumerate(
            [
                (band_hbm, band_ref),
                (weights_hbm, weights_ref),
                (slot_hbm, slot_ref),
                (prior_hbm.at[0], own.at[0]),
                (dens_hbm.at[0], own.at[1]),
                (cot_hbm.at[0], cot),
                (bary_hbm, bary),
            ]
        )
    ]
    for load in loads:
        load.start()

    barrier = pltpu.get_barrier_semaphore()

    @pl.loop(1, slabs)
    def _(k):
        pl.semaphore_signal(
            barrier, inc=1, device_id=(atom, lax.rem(me + k, slabs)), device_id_type=MESH
        )

    @pl.loop(1, atoms)
    def _(k):
        pl.semaphore_signal(
            barrier, inc=1, device_id=(lax.rem(atom + k, atoms), me), device_id_type=MESH
        )

    def rows_of(c):
        return pl.ds(pl.multiple_of(c * ROWS, ROWS), ROWS)

    def halo_copy(stage, way, c):
        first = planes - reach if way == 0 else 0
        return pltpu.make_async_remote_copy(
            src_ref=own.at[stage, pl.ds(first, reach), rows_of(c), :],
            dst_ref=halo.at[stage, way, :, rows_of(c), :],
            send_sem=hsend.at[stage, way, c],
            recv_sem=hrecv.at[stage, way, c],
            device_id=(atom, right if way == 0 else left),
            device_id_type=MESH,
        )

    def msg_copy(slot, way):
        return pltpu.make_async_remote_copy(
            src_ref=mine.at[slot],
            dst_ref=msg.at[slot, way],
            send_sem=msend.at[slot, way],
            recv_sem=mrecv.at[slot, way],
            device_id=(atom, right if way == 0 else left),
            device_id_type=MESH,
        )

    def cot_copy(c):
        return pltpu.make_async_remote_copy(
            src_ref=cot_hbm.at[0, :, rows_of(c), :],
            dst_ref=other.at[:, rows_of(c), :],
            send_sem=csend.at[c],
            recv_sem=crecv.at[c],
            device_id=(1 - atom, me),
            device_id_type=MESH,
        )

    def part_copy(source, target):
        return pltpu.make_async_remote_copy(
            src_ref=slab_parts.at[me],
            dst_ref=slab_parts.at[source],
            send_sem=psend.at[target],
            recv_sem=precv.at[source],
            device_id=(atom, target),
            device_id_type=MESH,
        )

    def atom_copy(source, target):
        return pltpu.make_async_remote_copy(
            src_ref=atom_parts.at[atom],
            dst_ref=atom_parts.at[source],
            send_sem=asend.at[target],
            recv_sem=arecv.at[source],
            device_id=(target, me),
            device_id_type=MESH,
        )

    there = (has_right, has_left)
    comes = (has_left, has_right)

    def send(stage, c):
        for way in range(2):
            @pl.when(there[way])
            def _():
                halo_copy(stage, way, c).start()

    def send_msg(slot, value):
        mine[slot] = jnp.full((8, 128), value, F32)
        for way in range(2):
            @pl.when(there[way])
            def _():
                msg_copy(slot, way).start()

    def take_msg(slot):
        for way in range(2):
            @pl.when(comes[way])
            def _():
                msg_copy(slot, way).wait_recv()

            @pl.when(jnp.logical_not(comes[way]))
            def _():
                msg[slot, way] = mine[slot]
        return jnp.max(msg[slot, 0]), jnp.max(msg[slot, 1])

    def zx(stage, c):
        for way in range(2):
            @pl.when(comes[way])
            def _():
                halo_copy(stage, way, c).wait_recv()

        tiles = cols // 128

        @pl.loop(0, tiles * (ROWS // 8))
        def _(t):
            r = pl.multiple_of((t // tiles) * 8, 8)
            at = pl.ds(pl.multiple_of(c * ROWS + r, 8), 8)
            lanes = pl.ds(pl.multiple_of((t % tiles) * 128, 128), 128)
            e = [halo[stage, 0, p, at, lanes] * fac[0, c] for p in range(reach)]
            e += [own[stage, p, at, lanes] * fac[1, c] for p in range(planes)]
            e += [halo[stage, 1, p, at, lanes] * fac[2, c] for p in range(reach)]
            for p in range(planes):
                total = e[p + reach] * wz[0]
                for k in range(1, reach + 1):
                    total = total + (e[p + reach - k] + e[p + reach + k]) * wz[k]
                zbuf[p, pl.ds(r, 8), lanes] = total

        high, low = split(zbuf[...].reshape(planes * ROWS, cols))
        both = dot(jnp.concatenate([high, low], axis=0), kx[0])
        res = both[: planes * ROWS] + (both[planes * ROWS :] + dot(high, kx[1]))
        res = res.reshape(planes, ROWS, cols)
        xbuf[:, pl.ds(pl.multiple_of(c * ROWS + 8, 8), ROWS), :] = res

    def yy(c):
        around = pl.ds(pl.multiple_of(c * ROWS, ROWS), 2 * ROWS)
        for part in range(planes // 8):
            high, low = split(xbuf[part * 8 : part * 8 + 8, around, :].reshape(16 * ROWS, cols))
            both = dot(ky[...].reshape(16 * ROWS, 16 * ROWS), high)
            res = both[: 8 * ROWS] + (both[8 * ROWS :] + dot(ky[0], low))
            ybuf[part * 8 : part * 8 + 8] = res.reshape(8, ROWS, cols)

    def run(stage, post):
        @pl.loop(0, chunks + 1)
        def _(c):
            @pl.when(c < chunks)
            def _():
                zx(stage, c)

            @pl.when(c > 0)
            def _():
                yy(c - 1)
                post(c - 1)

    def factor(a, b):
        return jnp.exp(jnp.full((8, 128), a - b, F32))

    def set_factors(values):
        for way, value in enumerate(values):
            for c in range(chunks):
                fac[way, c] = value

    pl.semaphore_wait(barrier, slabs - 1 + atoms - 1)
    if swap:
        @pl.loop(0, chunks)
        def _(c):
            cot_copy(c).start()

    loads[3].wait()
    zmax[...] = jnp.full((8, cols), -jnp.inf, F32)

    @pl.loop(0, planes)
    def _(p):
        zmax[...] = jnp.maximum(zmax[...], jnp.max(own[0, p].reshape(rows // 8, 8, cols), axis=0))

    m1 = jnp.max(zmax[...])
    send_msg(0, m1)

    @pl.loop(0, chunks)
    def _(c):
        @pl.loop(0, planes)
        def _(p):
            own[0, p, rows_of(c), :] = jnp.exp(own[0, p, rows_of(c), :] - m1)

        send(0, c)

    for load in loads[:3]:
        load.wait()

    d = lax.broadcasted_iota(jnp.int32, (cols, cols), 0) - lax.broadcasted_iota(jnp.int32, (cols, cols), 1)
    kx[0], kx[1] = split(jnp.where(jnp.abs(d) <= band_ref[0], tap(d), 0.0))
    i = lax.broadcasted_iota(jnp.int32, (8 * ROWS, 16 * ROWS), 0)
    j = lax.broadcasted_iota(jnp.int32, (8 * ROWS, 16 * ROWS), 1)
    d = (j & (2 * ROWS - 1)) - ROWS // 2 - (i & (ROWS - 1))
    same = (i // ROWS) == (j // (2 * ROWS))
    ky[0], ky[1] = split(jnp.where(same & (jnp.abs(d) <= band_ref[1]), tap(d), 0.0))
    xbuf[:, 0:8, :] = jnp.zeros((planes, 8, cols), F32)
    xbuf[:, rows + 8 : rows + 16, :] = jnp.zeros((planes, 8, cols), F32)
    part_ref[...] = jnp.zeros(part_ref.shape, F32)
    for way in range(2):
        @pl.when(jnp.logical_not(comes[way]))
        def _():
            @pl.loop(0, 3)
            def _(stage):
                @pl.loop(0, reach)
                def _(p):
                    halo[stage, way, p] = jnp.zeros((rows, cols), F32)

    half = band_ref[2]
    wz = [
        jnp.where(half >= k, tap(jnp.full((8, 128), k, jnp.int32)), 0.0)
        for k in range(reach + 1)
    ]

    m1_left, m1_right = take_msg(0)
    c1 = jnp.maximum(m1, jnp.maximum(m1_left, m1_right))
    loads[4].wait()

    def post1(c):
        zmax[...] = jnp.full((8, cols), -jnp.inf, F32)

        @pl.loop(0, planes)
        def _(p):
            potential = own[1, p, rows_of(c), :] - (jnp.log(ybuf[p]) + c1)
            own[1, p, rows_of(c), :] = potential
            zmax[...] = jnp.maximum(zmax[...], jnp.max(potential.reshape(ROWS // 8, 8, cols), axis=0))

        m = jnp.max(zmax[...])
        send_msg(c + 1, m)

        @pl.loop(0, planes)
        def _(p):
            own[1, p, rows_of(c), :] = jnp.exp(own[1, p, rows_of(c), :] - m)

        send(1, c)

    set_factors([factor(m1_left, c1), factor(m1, c1), factor(m1_right, c1)])
    run(0, post1)

    m2s = [jnp.max(mine[c + 1]) for c in range(chunks)]
    around = [take_msg(c + 1) for c in range(chunks)]
    m2 = functools.reduce(jnp.maximum, m2s)
    c2 = functools.reduce(jnp.maximum, [v for pair in around for v in pair], m2)
    send_msg(chunks + 1, c2)
    for c in range(chunks):
        fac[0, c] = factor(around[c][0], c2)
        fac[1, c] = factor(m2s[c], c2)
        fac[2, c] = factor(around[c][1], c2)
        fin[c] = factor(m2s[c], m2)
    weight = weights_ref[slot_ref[atom]]
    loads[5].wait()
    loads[6].wait()

    def post2(c):
        if swap:
            cot_copy(c).wait_recv()

        @pl.loop(0, planes)
        def _(p):
            cot_here = cot[p, rows_of(c), :]
            summed = bary[p, rows_of(c), :]
            if swap:
                summed = summed + (cot_here + other[p, rows_of(c), :])
            second = ybuf[p]
            product = summed * (jnp.log(second) + c2)
            part_ref[...] += jnp.sum(product.reshape(ROWS // 8, 8, cols), axis=0)
            own[2, p, rows_of(c), :] = (weight * summed - cot_here) / second

        send(2, c)

    run(1, post2)

    slab_parts[me] = sum(part_ref[:, k * 128 : (k + 1) * 128] for k in range(cols // 128))

    @pl.loop(1, slabs)
    def _(k):
        part_copy(me, lax.rem(me + k, slabs)).start()

    def share():
        @pl.loop(1, slabs)
        def _(k):
            other_slab = lax.rem(me + k, slabs)
            part_copy(other_slab, other_slab).wait_recv()

        atom_parts[atom] = jnp.sum(slab_parts[...], axis=0) / (slabs * planes * rows * cols)

        @pl.loop(1, atoms)
        def _(k):
            atom_copy(atom, lax.rem(atom + k, atoms)).start()

    c2_left, c2_right = take_msg(chunks + 1)
    set_factors([factor(m2, c2_left), factor(m2, c2), factor(m2, c2_right)])

    def out_copy(c):
        return pltpu.make_async_copy(
            obuf.at[:, rows_of(c), :], out_hbm.at[0, :, rows_of(c), :], out_sem.at[c]
        )

    def post3(c):
        scale = jnp.max(fin[c])

        @pl.loop(0, planes)
        def _(p):
            obuf[p, rows_of(c), :] = (own[1, p, rows_of(c), :] * scale) * ybuf[p]

        out_copy(c).start()

        @pl.when(c == chunks - 2)
        def _():
            share()

    run(2, post3)

    @pl.loop(0, chunks)
    def _(c):
        out_copy(c).wait()
        if swap:
            cot_copy(c).wait_send()
        for stage in range(3):
            for way in range(2):
                @pl.when(there[way])
                def _():
                    halo_copy(stage, way, c).wait_send()

    @pl.loop(0, chunks + 2)
    def _(slot):
        for way in range(2):
            @pl.when(there[way])
            def _():
                msg_copy(slot, way).wait_send()

    @pl.loop(1, slabs)
    def _(k):
        target = lax.rem(me + k, slabs)
        part_copy(me, target).wait_send()

    @pl.loop(1, atoms)
    def _(k):
        other_atom = lax.rem(atom + k, atoms)
        atom_copy(atom, other_atom).wait_send()
        atom_copy(other_atom, other_atom).wait_recv()

    totals = [jnp.sum(atom_parts[k]) for k in range(atoms)]
    for j in range(atoms):
        wgrad_ref[j] = sum(jnp.where(slot_ref[k] == j, totals[k], 0.0) for k in range(atoms))


def body(dens, prior, cot, bary, weights, band, slot_atom_index):
    swap = lax.axis_size("atom") == 2
    if not swap:
        bary = bary + lax.psum(cot[0], "atom")
    steps = BAND_MAX // STEP
    which = sum((band[2] > STEP * k).astype(jnp.int32) for k in range(1, steps))
    return lax.switch(
        which,
        [functools.partial(reverse, STEP * (k + 1)) for k in range(steps)],
        dens, prior, cot, bary, weights, band, slot_atom_index,
    )


def reverse(reach, dens, prior, cot, bary, weights, band, slot_atom_index):
    held = dens.shape[0]
    assert held == 1
    planes, rows, cols = bary.shape
    slabs = lax.axis_size("slab")
    atoms = lax.axis_size("atom")
    swap = atoms == 2
    chunks = rows // ROWS
    dma = pltpu.SemaphoreType.DMA
    full = pltpu.VMEM((planes, rows, cols), F32)
    return pl.pallas_call(
        functools.partial(kernel, reach, swap, atoms, slabs, planes, rows, cols),
        out_shape=(
            jax.ShapeDtypeStruct(dens.shape, F32),
            jax.ShapeDtypeStruct((atoms,), F32),
        ),
        in_specs=[pl.BlockSpec(memory_space=pl.ANY)] * 7,
        out_specs=(pl.BlockSpec(memory_space=pl.ANY), pl.BlockSpec(memory_space=pltpu.SMEM)),
        scratch_shapes=[
            pltpu.VMEM((3, planes, rows, cols), F32),
            pltpu.VMEM((3, 2, reach, rows, cols), F32),
            full,
            full,
            full,
            pltpu.VMEM((planes, rows + 16, cols), F32),
            pltpu.VMEM((planes, ROWS, cols), F32),
            pltpu.VMEM((planes, ROWS, cols), F32),
            full,
            pltpu.VMEM((chunks + 2, 8, 128), F32),
            pltpu.VMEM((chunks + 2, 2, 8, 128), F32),
            pltpu.VMEM((2, cols, cols), BF16),
            pltpu.VMEM((2, 8 * ROWS, 16 * ROWS), BF16),
            pltpu.VMEM((8, cols), F32),
            pltpu.VMEM((8, cols), F32),
            pltpu.VMEM((slabs, 8, 128), F32),
            pltpu.VMEM((atoms, 8, 128), F32),
            pltpu.SMEM((atoms,), F32),
            pltpu.SMEM((3,), jnp.int32),
            pltpu.SMEM((atoms,), jnp.int32),
            pltpu.VMEM((3, chunks, 8, 128), F32),
            pltpu.VMEM((chunks, 8, 128), F32),
            dma((7,)),
            dma((chunks,)),
            dma((3, 2, chunks)),
            dma((3, 2, chunks)),
            dma((chunks + 2, 2)),
            dma((chunks + 2, 2)),
            dma((chunks,)),
            dma((chunks,)),
            dma((slabs,)),
            dma((slabs,)),
            dma((atoms,)),
            dma((atoms,)),
        ],
        compiler_params=pltpu.CompilerParams(
            collective_id=reach, has_side_effects=True, vmem_limit_bytes=52 * 1024 * 1024
        ),
        name=f"sinkhorn_reach_{reach}",
    )(dens, prior, cot, bary, weights, band, slot_atom_index)


def solution(mesh):
    return jax.shard_map(
        body,
        mesh=mesh,
        in_specs=(
            P("atom", "slab", None, None),
            P("atom", "slab", None, None),
            P("atom", "slab", None, None),
            P("slab", None, None),
            P(),
            P(),
            P(),
        ),
        out_specs=(P("atom", "slab", None, None), P()),
        check_vma=False,
    )
```

```python
import functools

import jax
import jax.numpy as jnp
from jax import lax
from jax.experimental import pallas as pl
from jax.experimental.pallas import tpu as pltpu
from jax.sharding import PartitionSpec as P

BAND_MAX = 8
ROWS = 16
STEP = 2
MESH = pl.DeviceIdType.MESH
F32 = jnp.float32
BF16 = jnp.bfloat16


def tap(offset):
    spread = offset.astype(F32)
    return jnp.exp(-2.0 * spread * spread / (BAND_MAX * BAND_MAX))


def split(value):
    high = value.astype(BF16)
    return high, (value - high.astype(F32)).astype(BF16)


def dot(a, b):
    return jnp.dot(a, b, preferred_element_type=F32)


def kernel(
    reach, swap, atoms, slabs, planes, rows, cols,
    dens_hbm, prior_hbm, cot_hbm, bary_hbm, weights_hbm, band_hbm, slot_hbm,
    out_hbm, wgrad_ref,
    own, halo, cot, bary, other, xbuf, zbuf, ybuf, obuf, mine, msg, kx, ky, zmax, part_ref, slab_parts, atom_parts,
    weights_ref, band_ref, slot_ref, fac, fin,
    load_sem, out_sem, hsend, hrecv, msend, mrecv, csend, crecv, psend, precv, asend, arecv,
):
    chunks = rows // ROWS
    me = lax.axis_index("slab")
    atom = lax.axis_index("atom")
    right = lax.rem(me + 1, slabs)
    left = lax.rem(me + slabs - 1, slabs)
    has_left = me > 0
    has_right = me < slabs - 1

    loads = [
        pltpu.make_async_copy(src, dst, load_sem.at[i])
        for i, (src, dst) in enumerate(
            [
                (band_hbm, band_ref),
                (weights_hbm, weights_ref),
                (slot_hbm, slot_ref),
                (prior_hbm.at[0], own.at[0]),
                (dens_hbm.at[0], own.at[1]),
                (cot_hbm.at[0], cot),
                (bary_hbm, bary),
            ]
        )
    ]
    for load in loads:
        load.start()

    barrier = pltpu.get_barrier_semaphore()

    @pl.loop(1, slabs)
    def _(k):
        pl.semaphore_signal(
            barrier, inc=1, device_id=(atom, lax.rem(me + k, slabs)), device_id_type=MESH
        )

    @pl.loop(1, atoms)
    def _(k):
        pl.semaphore_signal(
            barrier, inc=1, device_id=(lax.rem(atom + k, atoms), me), device_id_type=MESH
        )

    def rows_of(c):
        return pl.ds(pl.multiple_of(c * ROWS, ROWS), ROWS)

    def halo_copy(stage, way, c):
        first = planes - reach if way == 0 else 0
        return pltpu.make_async_remote_copy(
            src_ref=own.at[stage, pl.ds(first, reach), rows_of(c), :],
            dst_ref=halo.at[stage, way, :, rows_of(c), :],
            send_sem=hsend.at[stage, way, c],
            recv_sem=hrecv.at[stage, way, c],
            device_id=(atom, right if way == 0 else left),
            device_id_type=MESH,
        )

    def msg_copy(slot, way):
        return pltpu.make_async_remote_copy(
            src_ref=mine.at[slot],
            dst_ref=msg.at[slot, way],
            send_sem=msend.at[slot, way],
            recv_sem=mrecv.at[slot, way],
            device_id=(atom, right if way == 0 else left),
            device_id_type=MESH,
        )

    def cot_copy(c):
        return pltpu.make_async_remote_copy(
            src_ref=cot_hbm.at[0, :, rows_of(c), :],
            dst_ref=other.at[:, rows_of(c), :],
            send_sem=csend.at[c],
            recv_sem=crecv.at[c],
            device_id=(1 - atom, me),
            device_id_type=MESH,
        )

    def part_copy(source, target):
        return pltpu.make_async_remote_copy(
            src_ref=slab_parts.at[me],
            dst_ref=slab_parts.at[source],
            send_sem=psend.at[target],
            recv_sem=precv.at[source],
            device_id=(atom, target),
            device_id_type=MESH,
        )

    def atom_copy(source, target):
        return pltpu.make_async_remote_copy(
            src_ref=atom_parts.at[atom],
            dst_ref=atom_parts.at[source],
            send_sem=asend.at[target],
            recv_sem=arecv.at[source],
            device_id=(target, me),
            device_id_type=MESH,
        )

    there = (has_right, has_left)
    comes = (has_left, has_right)

    def send(stage, c):
        for way in range(2):
            @pl.when(there[way])
            def _():
                halo_copy(stage, way, c).start()

    def send_msg(slot, value):
        mine[slot] = jnp.full((8, 128), value, F32)
        for way in range(2):
            @pl.when(there[way])
            def _():
                msg_copy(slot, way).start()

    def take_msg(slot):
        for way in range(2):
            @pl.when(comes[way])
            def _():
                msg_copy(slot, way).wait_recv()

            @pl.when(jnp.logical_not(comes[way]))
            def _():
                msg[slot, way] = mine[slot]
        return jnp.max(msg[slot, 0]), jnp.max(msg[slot, 1])

    def zx(stage, c):
        for way in range(2):
            @pl.when(comes[way])
            def _():
                halo_copy(stage, way, c).wait_recv()

        tiles = cols // 128

        @pl.loop(0, tiles * (ROWS // 8))
        def _(t):
            r = pl.multiple_of((t // tiles) * 8, 8)
            at = pl.ds(pl.multiple_of(c * ROWS + r, 8), 8)
            lanes = pl.ds(pl.multiple_of((t % tiles) * 128, 128), 128)
            e = [halo[stage, 0, p, at, lanes] * fac[0, c] for p in range(reach)]
            e += [own[stage, p, at, lanes] * fac[1, c] for p in range(planes)]
            e += [halo[stage, 1, p, at, lanes] * fac[2, c] for p in range(reach)]
            for p in range(planes):
                total = e[p + reach] * wz[0]
                for k in range(1, reach + 1):
                    total = total + (e[p + reach - k] + e[p + reach + k]) * wz[k]
                zbuf[p, pl.ds(r, 8), lanes] = total

        high, low = split(zbuf[...].reshape(planes * ROWS, cols))
        both = dot(jnp.concatenate([high, low], axis=0), kx[0])
        res = both[: planes * ROWS] + (both[planes * ROWS :] + dot(high, kx[1]))
        res = res.reshape(planes, ROWS, cols)
        xbuf[:, pl.ds(pl.multiple_of(c * ROWS + 8, 8), ROWS), :] = res

    def yy(c):
        around = pl.ds(pl.multiple_of(c * ROWS, ROWS), 2 * ROWS)
        for part in range(planes // 8):
            high, low = split(xbuf[part * 8 : part * 8 + 8, around, :].reshape(16 * ROWS, cols))
            both = dot(ky[...].reshape(16 * ROWS, 16 * ROWS), high)
            res = both[: 8 * ROWS] + (both[8 * ROWS :] + dot(ky[0], low))
            ybuf[part * 8 : part * 8 + 8] = res.reshape(8, ROWS, cols)

    def run(stage, post):
        @pl.loop(0, chunks + 1)
        def _(c):
            @pl.when(c < chunks)
            def _():
                zx(stage, c)

            @pl.when(c > 0)
            def _():
                yy(c - 1)
                post(c - 1)

    def factor(a, b):
        return jnp.exp(jnp.full((8, 128), a - b, F32))

    def set_factors(values):
        for way, value in enumerate(values):
            for c in range(chunks):
                fac[way, c] = value

    pl.semaphore_wait(barrier, slabs - 1 + atoms - 1)
    if swap:
        @pl.loop(0, chunks)
        def _(c):
            cot_copy(c).start()

    loads[3].wait()
    zmax[...] = jnp.full((8, cols), -jnp.inf, F32)

    @pl.loop(0, planes, unroll=4)
    def _(p):
        zmax[...] = jnp.maximum(zmax[...], jnp.max(own[0, p].reshape(rows // 8, 8, cols), axis=0))

    m1 = jnp.max(zmax[...])
    send_msg(0, m1)

    @pl.loop(0, chunks)
    def _(c):
        @pl.loop(0, planes, unroll=4)
        def _(p):
            own[0, p, rows_of(c), :] = jnp.exp(own[0, p, rows_of(c), :] - m1)

        send(0, c)

    for load in loads[:3]:
        load.wait()

    d = lax.broadcasted_iota(jnp.int32, (cols, cols), 0) - lax.broadcasted_iota(jnp.int32, (cols, cols), 1)
    kx[0], kx[1] = split(jnp.where(jnp.abs(d) <= band_ref[0], tap(d), 0.0))
    i = lax.broadcasted_iota(jnp.int32, (8 * ROWS, 16 * ROWS), 0)
    j = lax.broadcasted_iota(jnp.int32, (8 * ROWS, 16 * ROWS), 1)
    d = (j & (2 * ROWS - 1)) - ROWS // 2 - (i & (ROWS - 1))
    same = (i // ROWS) == (j // (2 * ROWS))
    ky[0], ky[1] = split(jnp.where(same & (jnp.abs(d) <= band_ref[1]), tap(d), 0.0))
    xbuf[:, 0:8, :] = jnp.zeros((planes, 8, cols), F32)
    xbuf[:, rows + 8 : rows + 16, :] = jnp.zeros((planes, 8, cols), F32)
    part_ref[...] = jnp.zeros(part_ref.shape, F32)
    for way in range(2):
        @pl.when(jnp.logical_not(comes[way]))
        def _():
            @pl.loop(0, 3)
            def _(stage):
                @pl.loop(0, reach)
                def _(p):
                    halo[stage, way, p] = jnp.zeros((rows, cols), F32)

    half = band_ref[2]
    wz = [
        jnp.where(half >= k, tap(jnp.full((8, 128), k, jnp.int32)), 0.0)
        for k in range(reach + 1)
    ]

    m1_left, m1_right = take_msg(0)
    c1 = jnp.maximum(m1, jnp.maximum(m1_left, m1_right))
    loads[4].wait()

    def post1(c):
        zmax[...] = jnp.full((8, cols), -jnp.inf, F32)

        @pl.loop(0, planes, unroll=4)
        def _(p):
            potential = own[1, p, rows_of(c), :] - (jnp.log(ybuf[p]) + c1)
            own[1, p, rows_of(c), :] = potential
            zmax[...] = jnp.maximum(zmax[...], jnp.max(potential.reshape(ROWS // 8, 8, cols), axis=0))

        m = jnp.max(zmax[...])
        send_msg(c + 1, m)

        @pl.loop(0, planes, unroll=4)
        def _(p):
            own[1, p, rows_of(c), :] = jnp.exp(own[1, p, rows_of(c), :] - m)

        send(1, c)

    set_factors([factor(m1_left, c1), factor(m1, c1), factor(m1_right, c1)])
    run(0, post1)

    m2s = [jnp.max(mine[c + 1]) for c in range(chunks)]
    around = [take_msg(c + 1) for c in range(chunks)]
    m2 = functools.reduce(jnp.maximum, m2s)
    c2 = functools.reduce(jnp.maximum, [v for pair in around for v in pair], m2)
    send_msg(chunks + 1, c2)
    for c in range(chunks):
        fac[0, c] = factor(around[c][0], c2)
        fac[1, c] = factor(m2s[c], c2)
        fac[2, c] = factor(around[c][1], c2)
        fin[c] = factor(m2s[c], m2)
    weight = weights_ref[slot_ref[atom]]
    loads[5].wait()
    loads[6].wait()

    def post2(c):
        if swap:
            cot_copy(c).wait_recv()

        @pl.loop(0, planes, unroll=4)
        def _(p):
            cot_here = cot[p, rows_of(c), :]
            summed = bary[p, rows_of(c), :]
            if swap:
                summed = summed + (cot_here + other[p, rows_of(c), :])
            second = ybuf[p]
            product = summed * (jnp.log(second) + c2)
            part_ref[...] += jnp.sum(product.reshape(ROWS // 8, 8, cols), axis=0)
            own[2, p, rows_of(c), :] = (weight * summed - cot_here) / second

        send(2, c)

    run(1, post2)

    slab_parts[me] = sum(part_ref[:, k * 128 : (k + 1) * 128] for k in range(cols // 128))

    @pl.loop(1, slabs)
    def _(k):
        part_copy(me, lax.rem(me + k, slabs)).start()

    def share():
        @pl.loop(1, slabs)
        def _(k):
            other_slab = lax.rem(me + k, slabs)
            part_copy(other_slab, other_slab).wait_recv()

        atom_parts[atom] = jnp.sum(slab_parts[...], axis=0) / (slabs * planes * rows * cols)

        @pl.loop(1, atoms)
        def _(k):
            atom_copy(atom, lax.rem(atom + k, atoms)).start()

    c2_left, c2_right = take_msg(chunks + 1)
    set_factors([factor(m2, c2_left), factor(m2, c2), factor(m2, c2_right)])

    def out_copy(c):
        return pltpu.make_async_copy(
            obuf.at[:, rows_of(c), :], out_hbm.at[0, :, rows_of(c), :], out_sem.at[c]
        )

    def post3(c):
        scale = jnp.max(fin[c])

        @pl.loop(0, planes, unroll=4)
        def _(p):
            obuf[p, rows_of(c), :] = (own[1, p, rows_of(c), :] * scale) * ybuf[p]

        out_copy(c).start()

        @pl.when(c == chunks - 2)
        def _():
            share()

    run(2, post3)

    @pl.loop(0, chunks)
    def _(c):
        out_copy(c).wait()
        if swap:
            cot_copy(c).wait_send()
        for stage in range(3):
            for way in range(2):
                @pl.when(there[way])
                def _():
                    halo_copy(stage, way, c).wait_send()

    @pl.loop(0, chunks + 2)
    def _(slot):
        for way in range(2):
            @pl.when(there[way])
            def _():
                msg_copy(slot, way).wait_send()

    @pl.loop(1, slabs)
    def _(k):
        target = lax.rem(me + k, slabs)
        part_copy(me, target).wait_send()

    @pl.loop(1, atoms)
    def _(k):
        other_atom = lax.rem(atom + k, atoms)
        atom_copy(atom, other_atom).wait_send()
        atom_copy(other_atom, other_atom).wait_recv()

    totals = [jnp.sum(atom_parts[k]) for k in range(atoms)]
    for j in range(atoms):
        wgrad_ref[j] = sum(jnp.where(slot_ref[k] == j, totals[k], 0.0) for k in range(atoms))


def body(dens, prior, cot, bary, weights, band, slot_atom_index):
    swap = lax.axis_size("atom") == 2
    if not swap:
        bary = bary + lax.psum(cot[0], "atom")
    steps = BAND_MAX // STEP
    which = sum((band[2] > STEP * k).astype(jnp.int32) for k in range(1, steps))
    return lax.switch(
        which,
        [functools.partial(reverse, STEP * (k + 1)) for k in range(steps)],
        dens, prior, cot, bary, weights, band, slot_atom_index,
    )


def reverse(reach, dens, prior, cot, bary, weights, band, slot_atom_index):
    held = dens.shape[0]
    assert held == 1
    planes, rows, cols = bary.shape
    slabs = lax.axis_size("slab")
    atoms = lax.axis_size("atom")
    swap = atoms == 2
    chunks = rows // ROWS
    dma = pltpu.SemaphoreType.DMA
    full = pltpu.VMEM((planes, rows, cols), F32)
    return pl.pallas_call(
        functools.partial(kernel, reach, swap, atoms, slabs, planes, rows, cols),
        out_shape=(
            jax.ShapeDtypeStruct(dens.shape, F32),
            jax.ShapeDtypeStruct((atoms,), F32),
        ),
        in_specs=[pl.BlockSpec(memory_space=pl.ANY)] * 7,
        out_specs=(pl.BlockSpec(memory_space=pl.ANY), pl.BlockSpec(memory_space=pltpu.SMEM)),
        scratch_shapes=[
            pltpu.VMEM((3, planes, rows, cols), F32),
            pltpu.VMEM((3, 2, reach, rows, cols), F32),
            full,
            full,
            full,
            pltpu.VMEM((planes, rows + 16, cols), F32),
            pltpu.VMEM((planes, ROWS, cols), F32),
            pltpu.VMEM((planes, ROWS, cols), F32),
            full,
            pltpu.VMEM((chunks + 2, 8, 128), F32),
            pltpu.VMEM((chunks + 2, 2, 8, 128), F32),
            pltpu.VMEM((2, cols, cols), BF16),
            pltpu.VMEM((2, 8 * ROWS, 16 * ROWS), BF16),
            pltpu.VMEM((8, cols), F32),
            pltpu.VMEM((8, cols), F32),
            pltpu.VMEM((slabs, 8, 128), F32),
            pltpu.VMEM((atoms, 8, 128), F32),
            pltpu.SMEM((atoms,), F32),
            pltpu.SMEM((3,), jnp.int32),
            pltpu.SMEM((atoms,), jnp.int32),
            pltpu.VMEM((3, chunks, 8, 128), F32),
            pltpu.VMEM((chunks, 8, 128), F32),
            dma((7,)),
            dma((chunks,)),
            dma((3, 2, chunks)),
            dma((3, 2, chunks)),
            dma((chunks + 2, 2)),
            dma((chunks + 2, 2)),
            dma((chunks,)),
            dma((chunks,)),
            dma((slabs,)),
            dma((slabs,)),
            dma((atoms,)),
            dma((atoms,)),
        ],
        compiler_params=pltpu.CompilerParams(
            collective_id=reach, has_side_effects=True, vmem_limit_bytes=52 * 1024 * 1024
        ),
        name=f"sinkhorn_reach_{reach}",
    )(dens, prior, cot, bary, weights, band, slot_atom_index)


def solution(mesh):
    return jax.shard_map(
        body,
        mesh=mesh,
        in_specs=(
            P("atom", "slab", None, None),
            P("atom", "slab", None, None),
            P("atom", "slab", None, None),
            P("slab", None, None),
            P(),
            P(),
            P(),
        ),
        out_specs=(P("atom", "slab", None, None), P()),
        check_vma=False,
    )
```
